512 devices in a mesh: rep: 16 (over y_hi, x, core), fsdp: 32 (over z, y_lo).
Axes of the slice: x: 4, y: 8 (y_hi: 2, y_lo: 4; y = y_hi * 4 + y_lo), z: 8, core: 2. Of those that a mesh axis runs over, the one named last changes fastest.
Arguments:
- grads: float32 [16, 256, 16384], P('rep', 'fsdp'), may hold values from -6 to 6
- master: float32 [256, 16384], P('fsdp'), may hold values from -6 to 6
- moment_one: float32 [256, 16384], P('fsdp'), may hold values from -2 to 2
- moment_two: float32 [256, 16384], P('fsdp'), may hold values from 0.05 to 2
Outputs:
- new_master: float32 [256, 16384], P('fsdp')
- new_one: float32 [256, 16384], P('fsdp')
- new_two: float32 [256, 16384], P('fsdp')
- rollout: bfloat16 [256, 16384], P(None, 'fsdp')
The draws below stay inside these ranges and needn't reach their ends.
All inputs are finite; a program needn't handle non-finite values.
Results may differ from the reference program's by a relative error of at most 0.0025.
Values may be sent and summed in bfloat16 or wider, within the bound.
No kernel may reach another device: no remote copies, remote signals or barrier semaphores. Data moves between devices by JAX's collectives and lax.ppermute only.
A program may use at most 64 MiB of HBM per device.

```python
import math
import jax
import jax.numpy as jnp
from jax import lax

D = 16384
STEP = 10
ROWS = 256
N_REP = 16


def block_levels(key, shape, split, least, largest):
    loudness = 1.0
    for dim, shards_of in split:
        draws = jax.random.uniform(jax.random.fold_in(jax.random.fold_in(key, 6), dim), (shards_of,), jnp.float32, least / len(split), largest / len(split))
        loudness = loudness * jnp.repeat(jnp.exp(draws), shape[dim] // shards_of).reshape((-1,) + (1,) * (len(shape) - 1 - dim))
    return loudness


def normal_values(own_key, shape, scale, most, pieces=(), held_as=jnp.bfloat16):
    loudness = block_levels(own_key, shape, pieces, -0.22, 0.18) if pieces else 1.0
    entries = jax.random.normal(own_key, shape, jnp.float32) * scale * loudness
    return jnp.minimum(jnp.maximum(entries, -most), most).astype(held_as)


def setup_inputs(seed: int = 0) -> dict:
    key_of = jax.random.split(jax.random.key(seed), 5)
    return {
        "grads": normal_values(key_of[0], (N_REP, ROWS, D), 1.0, 6.0, ((0, 16), (1, 32)), jnp.float32),
        "master": normal_values(key_of[1], (ROWS, D), 1.0, 6.0, ((0, 32),), jnp.float32),
        "moment_one": normal_values(key_of[2], (ROWS, D), 0.3, 2.0, ((0, 32),), jnp.float32),
        "moment_two": jnp.clip(jnp.exp(math.log(2.0) - 3.6888794 * jax.random.uniform(key_of[3], (ROWS, D), jnp.float32) ** block_levels(key_of[3], (ROWS, D), ((0, 32),), -0.2, 0.2)), 0.05, 2.0),
    }


def adamw(mean_grad, master, moment_one, moment_two):
    new_one = 0.9 * moment_one + 0.1 * mean_grad
    new_two = 0.95 * moment_two + 0.05 * mean_grad * mean_grad
    corrected_one = new_one / (1.0 - 0.9 ** STEP)
    corrected_two = new_two / (1.0 - 0.95 ** STEP)
    new_master = master - 0.02 * (corrected_one / (jnp.sqrt(corrected_two) + 1e-08) + 0.1 * master)
    return (new_master, new_one, new_two)

def reference(grads, master, moment_one, moment_two):
    mean_grad = lax.optimization_barrier(jnp.sum(grads, axis=0)) / N_REP
    new_master, new_one, new_two = adamw(mean_grad, master, moment_one, moment_two)
    return (new_master, new_one, new_two, new_master.astype(jnp.bfloat16))
```

```python
import jax
import jax.numpy as jnp
from jax import lax
from jax.experimental import pallas as pl
from jax.experimental.pallas import tpu as pltpu
from jax.sharding import Mesh
from jax.sharding import PartitionSpec as P

STEP = 10
FSDP = ("z", "y_lo")
BF16, F32 = jnp.bfloat16, jnp.float32


def adamw(mean_grad, master, moment_one, moment_two):
    new_one = 0.9 * moment_one + 0.1 * mean_grad
    new_two = 0.95 * moment_two + 0.05 * mean_grad * mean_grad
    corrected_one = new_one / (1.0 - 0.9**STEP)
    corrected_two = new_two / (1.0 - 0.95**STEP)
    new_master = master - 0.02 * (corrected_one / (jnp.sqrt(corrected_two) + 1e-08) + 0.1 * master)
    return (new_master, new_one, new_two)


def finish(core, own, their, master, moment_one, moment_two):
    rows, width = master.shape
    part = own.shape[1]
    owners = width // part // 2
    steps = 8
    each = owners // steps

    def kernel(core_ref, own_ref, their_ref, master_ref, one_ref, two_ref, new_master_ref, new_one_ref, new_two_ref):
        first = core_ref[0] == 0
        for owner in range(each):
            lines = slice(owner * rows, (owner + 1) * rows)
            mine, others = own_ref[lines, :], their_ref[lines, :]
            for place in range(2):
                mean_grad = jnp.where(first, mine, others) if place == 0 else jnp.where(first, others, mine)
                columns = slice((2 * owner + place) * part, (2 * owner + place + 1) * part)
                new_master, new_one, new_two = adamw(
                    mean_grad, master_ref[:, columns], one_ref[:, columns], two_ref[:, columns]
                )
                new_master_ref[:, columns] = new_master
                new_one_ref[:, columns] = new_one
                new_two_ref[:, columns] = new_two

    halves = pl.BlockSpec((each * rows, part), lambda i: (i, 0))
    wholes = pl.BlockSpec((rows, width // steps), lambda i: (0, i))
    return pl.pallas_call(
        kernel,
        grid=(steps,),
        in_specs=[pl.BlockSpec(memory_space=pltpu.SMEM), halves, halves, wholes, wholes, wholes],
        out_specs=[wholes] * 3,
        out_shape=[jax.ShapeDtypeStruct((rows, width), F32)] * 3,
        cost_estimate=pl.CostEstimate(
            flops=20 * rows * width, bytes_accessed=7 * 4 * rows * width, transcendentals=rows * width
        ),
        name="finish",
    )(core.reshape(1), own, their, master, moment_one, moment_two)


def local(grads, master, moment_one, moment_two):
    rows, width = master.shape
    owners = lax.axis_size(FSDP)
    cores = lax.axis_size("core")
    rings = lax.axis_size("x")
    rep_count = cores * rings * lax.axis_size("y_hi")
    part = width // owners // cores
    core = lax.axis_index("core")
    other = [(i, cores - 1 - i) for i in range(cores)]

    def half(source, which):
        blocks = source.reshape(rows, owners, cores, part).transpose(1, 2, 0, 3)
        return lax.dynamic_index_in_dim(blocks, which, 1, keepdims=False)

    theirs = lax.ppermute(half(grads[0], 1 - core).astype(BF16), "core", other)
    chip = (half(grads[0], core) + theirs.astype(F32)).astype(BF16)
    ring = lax.all_to_all(
        jnp.broadcast_to(chip[None], (rings,) + chip.shape), "x", split_axis=0, concat_axis=0, tiled=True
    )
    line = ring.astype(F32).sum(0).astype(BF16)
    far = lax.ppermute(line, "y_hi", [(0, 1), (1, 0)])
    mean_half = (line.astype(F32) + far.astype(F32)) / rep_count

    mean_other = lax.ppermute(mean_half, "core", other)
    fresh, _, _ = adamw(mean_half, half(master, core), half(moment_one, core), half(moment_two, core))
    moved = lax.all_to_all(fresh.astype(BF16), FSDP, split_axis=0, concat_axis=0, tiled=True)
    moved = moved.reshape(owners * rows, part)
    moved_other = lax.ppermute(moved, "core", other)

    new_master, new_one, new_two = finish(
        core, mean_half.reshape(owners * rows, part), mean_other.reshape(owners * rows, part),
        master, moment_one, moment_two,
    )
    rollout = jnp.where(
        core == 0, jnp.concatenate([moved, moved_other], 1), jnp.concatenate([moved_other, moved], 1)
    )
    return (new_master, new_one, new_two, rollout)


def solution(mesh):
    devices = mesh.devices.reshape(2, 4, 2, 8, 4)
    chips = Mesh(devices, ("y_hi", "x", "core", "z", "y_lo"))
    rep = ("y_hi", "x", "core")
    placed = (P(rep, FSDP, None), P(FSDP, None), P(FSDP, None), P(FSDP, None))
    return jax.shard_map(
        local,
        mesh=chips,
        in_specs=placed,
        out_specs=(P(FSDP, None), P(FSDP, None), P(FSDP, None), P(None, FSDP)),
        check_vma=False,
    )
```

```python
import jax
import jax.numpy as jnp
from jax import lax
from jax.experimental import pallas as pl
from jax.experimental.pallas import tpu as pltpu
from jax.sharding import Mesh
from jax.sharding import PartitionSpec as P

STEP = 10
FSDP = ("z", "y_lo")
BF16, F32 = jnp.bfloat16, jnp.float32


def adamw(mean_grad, master, moment_one, moment_two):
    new_one = 0.9 * moment_one + 0.1 * mean_grad
    new_two = 0.95 * moment_two + 0.05 * mean_grad * mean_grad
    corrected_one = new_one * (1.0 / (1.0 - 0.9**STEP))
    corrected_two = new_two * (1.0 / (1.0 - 0.95**STEP))
    new_master = master - 0.02 * (corrected_one / (jnp.sqrt(corrected_two) + 1e-08) + 0.1 * master)
    return (new_master, new_one, new_two)


def finish(mean_grad, master, moment_one, moment_two):
    rows, width = master.shape
    cores, _, part = mean_grad.shape
    owners = width // part // cores
    steps = 4
    each = owners // steps

    def kernel(mean_ref, master_ref, one_ref, two_ref, new_master_ref, new_one_ref, new_two_ref):
        for owner in range(each):
            for place in range(cores):
                columns = slice((cores * owner + place) * part, (cores * owner + place + 1) * part)
                new_master, new_one, new_two = adamw(
                    mean_ref[place, owner * rows : (owner + 1) * rows, :],
                    master_ref[:, columns],
                    one_ref[:, columns],
                    two_ref[:, columns],
                )
                new_master_ref[:, columns] = new_master
                new_one_ref[:, columns] = new_one
                new_two_ref[:, columns] = new_two

    wholes = pl.BlockSpec((rows, width // steps), lambda i: (0, i))
    return pl.pallas_call(
        kernel,
        grid=(steps,),
        in_specs=[pl.BlockSpec((cores, each * rows, part), lambda i: (0, i, 0)), wholes, wholes, wholes],
        out_specs=[wholes] * 3,
        out_shape=[jax.ShapeDtypeStruct((rows, width), F32)] * 3,
        cost_estimate=pl.CostEstimate(
            flops=20 * rows * width, bytes_accessed=7 * 4 * rows * width, transcendentals=rows * width
        ),
        name="finish",
    )(mean_grad, master, moment_one, moment_two)


def pack(core, arrays, part):
    rows, width = arrays[0].shape
    owners = width // part // 2
    steps = 4
    each = owners // steps

    def kernel(core_ref, *refs):
        out_ref = refs[-1]
        for owner in range(each):
            start = pl.multiple_of(2 * owner * part + core_ref[0] * part, part)
            for k, ref in enumerate(refs[:-1]):
                out_ref[owner, k] = ref[:, pl.ds(start, part)]

    return pl.pallas_call(
        kernel,
        grid=(steps,),
        in_specs=[pl.BlockSpec(memory_space=pltpu.SMEM)]
        + [pl.BlockSpec((rows, width // steps), lambda i: (0, i))] * len(arrays),
        out_specs=pl.BlockSpec((each, len(arrays), rows, part), lambda i: (i, 0, 0, 0)),
        out_shape=jax.ShapeDtypeStruct((owners, len(arrays), rows, part), F32),
        cost_estimate=pl.CostEstimate(flops=0, bytes_accessed=6 * len(arrays) * rows * width, transcendentals=0),
        name="pack",
    )(core.reshape(1), *arrays)


def local(grads, master, moment_one, moment_two):
    rows, width = master.shape
    owners = lax.axis_size(FSDP)
    cores = lax.axis_size("core")
    rings = lax.axis_size("x")
    rep_count = cores * rings * lax.axis_size("y_hi")
    part = width // owners // cores
    core = lax.axis_index("core")

    chips = lax.all_gather(grads[0].astype(BF16), "core")
    chips = chips.reshape(cores, rows, owners, cores, part).transpose(0, 2, 3, 1, 4)
    chip = lax.dynamic_index_in_dim(chips, core, 2, keepdims=False).astype(F32).sum(0).astype(BF16)
    ring = lax.all_to_all(
        jnp.broadcast_to(chip[None], (rings,) + chip.shape), "x", split_axis=0, concat_axis=0, tiled=True
    )
    states = pack(core, (master, moment_one, moment_two), part)
    ring, states = lax.optimization_barrier((ring, states))
    line = ring.astype(F32).sum(0).astype(BF16)
    mean_half = lax.all_gather(line, "y_hi").astype(F32).sum(0) / rep_count

    fresh, _, _ = adamw(mean_half, states[:, 0], states[:, 1], states[:, 2])
    moved = lax.all_to_all(fresh.astype(BF16), FSDP, split_axis=0, concat_axis=0, tiled=True)
    mean_grad = lax.all_gather(mean_half.reshape(owners * rows, part), "core")
    new_master, new_one, new_two = finish(mean_grad, master, moment_one, moment_two)
    moved, new_master, new_one, new_two = lax.optimization_barrier((moved, new_master, new_one, new_two))
    rollout = lax.all_gather(moved.reshape(owners * rows, part), "core", axis=1, tiled=True)
    return (new_master, new_one, new_two, rollout)


def solution(mesh):
    devices = mesh.devices.reshape(2, 4, 2, 8, 4)
    chips = Mesh(devices, ("y_hi", "x", "core", "z", "y_lo"))
    rep = ("y_hi", "x", "core")
    placed = (P(rep, FSDP, None), P(FSDP, None), P(FSDP, None), P(FSDP, None))
    return jax.shard_map(
        local,
        mesh=chips,
        in_specs=placed,
        out_specs=(P(FSDP, None), P(FSDP, None), P(FSDP, None), P(None, FSDP)),
        check_vma=False,
    )
```

```python
import jax
import jax.numpy as jnp
from jax import lax
from jax.experimental import pallas as pl
from jax.experimental.pallas import tpu as pltpu
from jax.sharding import Mesh
from jax.sharding import PartitionSpec as P

STEP = 10
FSDP = ("z", "y_lo")
BF16, F32 = jnp.bfloat16, jnp.float32


def adamw(mean_grad, master, moment_one, moment_two):
    new_one = 0.9 * moment_one + 0.1 * mean_grad
    new_two = 0.95 * moment_two + 0.05 * mean_grad * mean_grad
    corrected_one = new_one * (1.0 / (1.0 - 0.9**STEP))
    corrected_two = new_two * (1.0 / (1.0 - 0.95**STEP))
    new_master = master - 0.02 * (corrected_one / (jnp.sqrt(corrected_two) + 1e-08) + 0.1 * master)
    return (new_master, new_one, new_two)


VMEM = pl.BlockSpec(memory_space=pltpu.VMEM)


def combine(chips, owners):
    cores, rows, width = chips.shape
    part = width // owners // cores

    def kernel(chips_ref, sum_ref):
        core = lax.axis_index("core")
        for owner in range(0, owners, 2):
            sums = []
            for k in range(2):
                columns = pl.ds(pl.multiple_of((cores * (owner + k) + core) * part, part), part)
                sums.append(chips_ref[0, :, columns].astype(F32) + chips_ref[1, :, columns].astype(F32))
            sum_ref[owner * rows : (owner + 2) * rows, :] = jnp.concatenate(sums, 0).astype(BF16)

    return pl.pallas_call(
        kernel,
        in_specs=[VMEM],
        out_specs=VMEM,
        out_shape=jax.ShapeDtypeStruct((owners * rows, part), BF16),
        compiler_params=pltpu.CompilerParams(vmem_limit_bytes=8 * 2**20),
        cost_estimate=pl.CostEstimate(flops=rows * width, bytes_accessed=5 * rows * width, transcendentals=0),
        name="combine",
    )(chips)


def begin(lines, master, moment_one, moment_two, rep_count):
    rows, width = master.shape
    _, tall, part = lines.shape
    owners = tall // rows
    cores = width // part // owners

    def kernel(lines_ref, master_ref, one_ref, two_ref, fresh_ref, mean_ref):
        core = lax.axis_index("core")
        for owner in range(0, owners, 2):
            pair = slice(owner * rows, (owner + 2) * rows)
            mean_grad = (lines_ref[0, pair, :].astype(F32) + lines_ref[1, pair, :].astype(F32)) / rep_count
            mean_ref[pair, :] = mean_grad
            news = []
            for k in range(2):
                columns = pl.ds(pl.multiple_of((cores * (owner + k) + core) * part, part), part)
                new_master, _, _ = adamw(
                    mean_grad[k * rows : (k + 1) * rows],
                    master_ref[:, columns],
                    one_ref[:, columns],
                    two_ref[:, columns],
                )
                news.append(new_master)
            fresh_ref[pair, :] = jnp.concatenate(news, 0).astype(BF16)

    return pl.pallas_call(
        kernel,
        in_specs=[VMEM] * 4,
        out_specs=[VMEM] * 2,
        out_shape=[jax.ShapeDtypeStruct((tall, part), BF16), jax.ShapeDtypeStruct((tall, part), F32)],
        compiler_params=pltpu.CompilerParams(vmem_limit_bytes=16 * 2**20),
        cost_estimate=pl.CostEstimate(
            flops=20 * tall * part, bytes_accessed=20 * tall * part, transcendentals=tall * part
        ),
        name="begin",
    )(lines, master, moment_one, moment_two)


def finish(mean_grad, master, moment_one, moment_two):
    rows, width = master.shape
    cores, _, part = mean_grad.shape
    owners = width // part // cores
    steps = 4
    each = owners // steps

    def kernel(mean_ref, master_ref, one_ref, two_ref, *refs):
        outs, (held, sems) = refs[:3], refs[3:]
        copies = []
        for step in range(steps):
            for owner in range(step * each, (step + 1) * each):
                for place in range(cores):
                    columns = slice((cores * owner + place) * part, (cores * owner + place + 1) * part)
                    news = adamw(
                        mean_ref[place, owner * rows : (owner + 1) * rows, :],
                        master_ref[:, columns],
                        one_ref[:, columns],
                        two_ref[:, columns],
                    )
                    for k in range(3):
                        held[k, :, columns] = news[k]
            span = pl.ds(step * width // steps, width // steps)
            for k in range(3):
                copy = pltpu.make_async_copy(held.at[k, :, span], outs[k].at[:, span], sems.at[step, k])
                copy.start()
                copies.append(copy)
        for copy in copies:
            copy.wait()

    return pl.pallas_call(
        kernel,
        in_specs=[VMEM] * 4,
        out_specs=[pl.BlockSpec(memory_space=pl.ANY)] * 3,
        out_shape=[jax.ShapeDtypeStruct((rows, width), F32)] * 3,
        scratch_shapes=[pltpu.VMEM((3, rows, width), F32), pltpu.SemaphoreType.DMA((steps, 3))],
        compiler_params=pltpu.CompilerParams(vmem_limit_bytes=16 * 2**20),
        cost_estimate=pl.CostEstimate(
            flops=20 * rows * width, bytes_accessed=7 * 4 * rows * width, transcendentals=rows * width
        ),
        name="finish",
    )(mean_grad, master, moment_one, moment_two)


def local(grads, master, moment_one, moment_two):
    rows, width = master.shape
    owners = lax.axis_size(FSDP)
    cores = lax.axis_size("core")
    rep_count = cores * lax.axis_size("x") * lax.axis_size("y_hi")
    total = combine(lax.all_gather(grads[0].astype(BF16), "core"), owners)
    for pairs in ([[0, 1], [2, 3]], [[0, 3], [1, 2]]):
        total = lax.all_gather(total, "x", axis_index_groups=pairs).astype(F32).sum(0).astype(BF16)
    lines = lax.all_gather(total, "y_hi")

    fresh, mean_half = begin(lines, master, moment_one, moment_two, rep_count)
    moved = lax.all_to_all(fresh.reshape(owners, rows, -1), FSDP, split_axis=0, concat_axis=0, tiled=True)
    mean_grad = lax.all_gather(mean_half, "core")
    new_master, new_one, new_two = finish(mean_grad, master, moment_one, moment_two)
    moved, new_master, new_one, new_two = lax.optimization_barrier((moved, new_master, new_one, new_two))
    rollout = lax.all_gather(moved.reshape(fresh.shape), "core", axis=1, tiled=True)
    return (new_master, new_one, new_two, rollout)


def solution(mesh):
    devices = mesh.devices.reshape(2, 4, 2, 8, 4)
    chips = Mesh(devices, ("y_hi", "x", "core", "z", "y_lo"))
    rep = ("y_hi", "x", "core")
    placed = (P(rep, FSDP, None), P(FSDP, None), P(FSDP, None), P(FSDP, None))
    return jax.shard_map(
        local,
        mesh=chips,
        in_specs=placed,
        out_specs=(P(FSDP, None), P(FSDP, None), P(FSDP, None), P(None, FSDP)),
        check_vma=False,
    )
```

```python
import jax
import jax.numpy as jnp
from jax import lax
from jax.experimental import pallas as pl
from jax.experimental.pallas import tpu as pltpu
from jax.sharding import Mesh
from jax.sharding import PartitionSpec as P

STEP = 10
FSDP = ("z", "y_lo")
BF16, F32 = jnp.bfloat16, jnp.float32


def adamw(mean_grad, master, moment_one, moment_two):
    new_one = 0.9 * moment_one + 0.1 * mean_grad
    new_two = 0.95 * moment_two + 0.05 * mean_grad * mean_grad
    corrected_one = new_one * (1.0 / (1.0 - 0.9**STEP))
    corrected_two = new_two * (1.0 / (1.0 - 0.95**STEP))
    new_master = master - 0.02 * (corrected_one / (jnp.sqrt(corrected_two) + 1e-08) + 0.1 * master)
    return (new_master, new_one, new_two)


VMEM = pl.BlockSpec(memory_space=pltpu.VMEM)


def combine(chips, owners):
    cores, rows, width = chips.shape
    part = width // owners // cores

    def kernel(chips_ref, sum_ref):
        core = lax.axis_index("core")
        for owner in range(0, owners, 2):
            sums = []
            for k in range(2):
                columns = pl.ds(pl.multiple_of((cores * (owner + k) + core) * part, part), part)
                sums.append(chips_ref[0, :, columns].astype(F32) + chips_ref[1, :, columns].astype(F32))
            sum_ref[owner * rows : (owner + 2) * rows, :] = jnp.concatenate(sums, 0).astype(BF16)

    return pl.pallas_call(
        kernel,
        in_specs=[VMEM],
        out_specs=VMEM,
        out_shape=jax.ShapeDtypeStruct((owners * rows, part), BF16),
        compiler_params=pltpu.CompilerParams(vmem_limit_bytes=8 * 2**20),
        cost_estimate=pl.CostEstimate(flops=rows * width, bytes_accessed=5 * rows * width, transcendentals=0),
        name="combine",
    )(chips)


def begin(lines, master, moment_one, moment_two, rep_count):
    rows, width = master.shape
    _, tall, part = lines.shape
    owners = tall // rows
    cores = width // part // owners

    def kernel(lines_ref, master_ref, one_ref, two_ref, fresh_ref, mean_ref):
        core = lax.axis_index("core")
        for owner in range(0, owners, 2):
            pair = slice(owner * rows, (owner + 2) * rows)
            mean_grad = (lines_ref[0, pair, :].astype(F32) + lines_ref[1, pair, :].astype(F32)) / rep_count
            mean_ref[pair, :] = mean_grad
            news = []
            for k in range(2):
                columns = pl.ds(pl.multiple_of((cores * (owner + k) + core) * part, part), part)
                new_master, _, _ = adamw(
                    mean_grad[k * rows : (k + 1) * rows],
                    master_ref[:, columns],
                    one_ref[:, columns],
                    two_ref[:, columns],
                )
                news.append(new_master)
            fresh_ref[pair, :] = jnp.concatenate(news, 0).astype(BF16)

    return pl.pallas_call(
        kernel,
        in_specs=[VMEM] * 4,
        out_specs=[VMEM] * 2,
        out_shape=[jax.ShapeDtypeStruct((tall, part), BF16), jax.ShapeDtypeStruct((tall, part), F32)],
        compiler_params=pltpu.CompilerParams(vmem_limit_bytes=16 * 2**20),
        cost_estimate=pl.CostEstimate(
            flops=20 * tall * part, bytes_accessed=20 * tall * part, transcendentals=tall * part
        ),
        name="begin",
    )(lines, master, moment_one, moment_two)


def finish(mean_grad, master, moment_one, moment_two):
    rows, width = master.shape
    cores, _, part = mean_grad.shape
    owners = width // part // cores
    steps = 4
    each = owners // steps

    def kernel(mean_ref, master_ref, one_ref, two_ref, *refs):
        outs, (held, sems) = refs[:3], refs[3:]
        copies = []
        for step in range(steps):
            for owner in range(step * each, (step + 1) * each):
                for place in range(cores):
                    columns = slice((cores * owner + place) * part, (cores * owner + place + 1) * part)
                    news = adamw(
                        mean_ref[place, owner * rows : (owner + 1) * rows, :],
                        master_ref[:, columns],
                        one_ref[:, columns],
                        two_ref[:, columns],
                    )
                    for k in range(3):
                        held[k, :, columns] = news[k]
            span = pl.ds(step * width // steps, width // steps)
            for k in range(3):
                copy = pltpu.make_async_copy(held.at[k, :, span], outs[k].at[:, span], sems.at[step, k])
                copy.start()
                copies.append(copy)
        for copy in copies:
            copy.wait()

    return pl.pallas_call(
        kernel,
        in_specs=[VMEM] * 4,
        out_specs=[pl.BlockSpec(memory_space=pl.ANY)] * 3,
        out_shape=[jax.ShapeDtypeStruct((rows, width), F32)] * 3,
        scratch_shapes=[pltpu.VMEM((3, rows, width), F32), pltpu.SemaphoreType.DMA((steps, 3))],
        compiler_params=pltpu.CompilerParams(vmem_limit_bytes=16 * 2**20),
        cost_estimate=pl.CostEstimate(
            flops=20 * rows * width, bytes_accessed=7 * 4 * rows * width, transcendentals=rows * width
        ),
        name="finish",
    )(mean_grad, master, moment_one, moment_two)


def local(grads, master, moment_one, moment_two):
    rows, width = master.shape
    owners = lax.axis_size(FSDP)
    cores = lax.axis_size("core")
    rep_count = cores * lax.axis_size("x") * lax.axis_size("y_hi")
    total = combine(lax.all_gather(grads[0].astype(BF16), "core"), owners)
    rep = ("y_hi", "x", "core")
    for step in zip((2, 6, 8), (8, 2, 6)):
        pairs = [[i, i ^ step[i % 2]] for i in range(rep_count) if i < i ^ step[i % 2]]
        lines = lax.all_gather(total, rep, axis_index_groups=pairs)
        total = lines.astype(F32).sum(0).astype(BF16)

    fresh, mean_half = begin(lines, master, moment_one, moment_two, rep_count)
    moved = lax.all_to_all(fresh.reshape(owners, rows, -1), FSDP, split_axis=0, concat_axis=0, tiled=True)
    mean_grad = lax.all_gather(mean_half, "core")
    new_master, new_one, new_two = finish(mean_grad, master, moment_one, moment_two)
    moved, new_master, new_one, new_two = lax.optimization_barrier((moved, new_master, new_one, new_two))
    rollout = lax.all_gather(moved.reshape(fresh.shape), "core", axis=1, tiled=True)
    return (new_master, new_one, new_two, rollout)


def solution(mesh):
    devices = mesh.devices.reshape(2, 4, 2, 8, 4)
    chips = Mesh(devices, ("y_hi", "x", "core", "z", "y_lo"))
    rep = ("y_hi", "x", "core")
    placed = (P(rep, FSDP, None), P(FSDP, None), P(FSDP, None), P(FSDP, None))
    return jax.shard_map(
        local,
        mesh=chips,
        in_specs=placed,
        out_specs=(P(FSDP, None), P(FSDP, None), P(FSDP, None), P(None, FSDP)),
        check_vma=False,
    )
```

```python
import jax
import jax.numpy as jnp
from jax import lax
from jax.experimental import pallas as pl
from jax.experimental.pallas import tpu as pltpu
from jax.sharding import Mesh
from jax.sharding import PartitionSpec as P

STEP = 10
FSDP = ("z", "y_lo")
BF16, F32 = jnp.bfloat16, jnp.float32


def adamw(mean_grad, master, moment_one, moment_two):
    new_one = 0.9 * moment_one + 0.1 * mean_grad
    new_two = 0.95 * moment_two + 0.05 * mean_grad * mean_grad
    corrected_one = new_one * (1.0 / (1.0 - 0.9**STEP))
    corrected_two = new_two * (1.0 / (1.0 - 0.95**STEP))
    new_master = master - 0.02 * (corrected_one / (jnp.sqrt(corrected_two) + 1e-08) + 0.1 * master)
    return (new_master, new_one, new_two)


VMEM = pl.BlockSpec(memory_space=pltpu.VMEM)
REP = ("y_hi", "x", "core")


def half_of(place):
    return (place + place // 2 + place // 8) % 2


def own_half():
    return (lax.axis_index("core") + lax.axis_index("x") + lax.axis_index("y_hi")) % 2


def combine(chips, owners):
    cores, rows, width = chips.shape
    part = width // owners // cores

    def kernel(chips_ref, sum_ref):
        half = own_half()
        for owner in range(0, owners, 2):
            sums = []
            for k in range(2):
                columns = pl.ds(pl.multiple_of((cores * (owner + k) + half) * part, part), part)
                sums.append(chips_ref[0, :, columns].astype(F32) + chips_ref[1, :, columns].astype(F32))
            sum_ref[owner * rows : (owner + 2) * rows, :] = jnp.concatenate(sums, 0).astype(BF16)

    return pl.pallas_call(
        kernel,
        in_specs=[VMEM],
        out_specs=VMEM,
        out_shape=jax.ShapeDtypeStruct((owners * rows, part), BF16),
        compiler_params=pltpu.CompilerParams(vmem_limit_bytes=8 * 2**20),
        cost_estimate=pl.CostEstimate(flops=rows * width, bytes_accessed=5 * rows * width, transcendentals=0),
        name="combine",
    )(chips)


def begin(lines, master, moment_one, moment_two, rep_count):
    rows, width = master.shape
    _, tall, part = lines.shape
    owners = tall // rows
    cores = width // part // owners

    def kernel(lines_ref, master_ref, one_ref, two_ref, fresh_ref, mean_ref):
        half = own_half()
        for owner in range(0, owners, 2):
            pair = slice(owner * rows, (owner + 2) * rows)
            mean_grad = (lines_ref[0, pair, :].astype(F32) + lines_ref[1, pair, :].astype(F32)) / rep_count
            mean_ref[pair, :] = mean_grad
            news = []
            for k in range(2):
                columns = pl.ds(pl.multiple_of((cores * (owner + k) + half) * part, part), part)
                new_master, _, _ = adamw(
                    mean_grad[k * rows : (k + 1) * rows],
                    master_ref[:, columns],
                    one_ref[:, columns],
                    two_ref[:, columns],
                )
                news.append(new_master)
            fresh_ref[pair, :] = jnp.concatenate(news, 0).astype(BF16)

    return pl.pallas_call(
        kernel,
        in_specs=[VMEM] * 4,
        out_specs=[VMEM] * 2,
        out_shape=[jax.ShapeDtypeStruct((tall, part), BF16), jax.ShapeDtypeStruct((tall, part), F32)],
        compiler_params=pltpu.CompilerParams(vmem_limit_bytes=16 * 2**20),
        cost_estimate=pl.CostEstimate(
            flops=20 * tall * part, bytes_accessed=20 * tall * part, transcendentals=tall * part
        ),
        name="begin",
    )(lines, master, moment_one, moment_two)


def finish(mean_grad, master, moment_one, moment_two):
    rows, width = master.shape
    cores, _, part = mean_grad.shape
    owners = width // part // cores
    steps = 4
    each = owners // steps

    def kernel(mean_ref, master_ref, one_ref, two_ref, *refs):
        outs, (held, sems) = refs[:3], refs[3:]
        copies = []
        for step in range(steps):
            for owner in range(step * each, (step + 1) * each):
                for place in range(cores):
                    columns = slice((cores * owner + place) * part, (cores * owner + place + 1) * part)
                    news = adamw(
                        mean_ref[place, owner * rows : (owner + 1) * rows, :],
                        master_ref[:, columns],
                        one_ref[:, columns],
                        two_ref[:, columns],
                    )
                    for k in range(3):
                        held[k, :, columns] = news[k]
            span = pl.ds(step * width // steps, width // steps)
            for k in range(3):
                copy = pltpu.make_async_copy(held.at[k, :, span], outs[k].at[:, span], sems.at[step, k])
                copy.start()
                copies.append(copy)
        for copy in copies:
            copy.wait()

    return pl.pallas_call(
        kernel,
        in_specs=[VMEM] * 4,
        out_specs=[pl.BlockSpec(memory_space=pl.ANY)] * 3,
        out_shape=[jax.ShapeDtypeStruct((rows, width), F32)] * 3,
        scratch_shapes=[pltpu.VMEM((3, rows, width), F32), pltpu.SemaphoreType.DMA((steps, 3))],
        compiler_params=pltpu.CompilerParams(vmem_limit_bytes=16 * 2**20),
        cost_estimate=pl.CostEstimate(
            flops=20 * rows * width, bytes_accessed=7 * 4 * rows * width, transcendentals=rows * width
        ),
        name="finish",
    )(mean_grad, master, moment_one, moment_two)


def local(grads, master, moment_one, moment_two):
    rows, width = master.shape
    owners = lax.axis_size(FSDP)
    cores = lax.axis_size("core")
    rep_count = cores * lax.axis_size("x") * lax.axis_size("y_hi")
    total = combine(lax.all_gather(grads[0].astype(BF16), "core"), owners)
    for step in zip((3, 7, 9), (9, 3, 7)):
        pairs = [[i, i ^ step[half_of(i)]] for i in range(rep_count) if i < i ^ step[half_of(i)]]
        lines = lax.all_gather(total, REP, axis_index_groups=pairs)
        total = lines.astype(F32).sum(0).astype(BF16)

    fresh, mean_half = begin(lines, master, moment_one, moment_two, rep_count)
    moved = lax.all_to_all(fresh.reshape(owners, rows, -1), FSDP, split_axis=0, concat_axis=0, tiled=True)
    chips = [[i + half_of(i), i + 1 - half_of(i)] for i in range(0, rep_count, 2)]
    mean_grad = lax.all_gather(mean_half, REP, axis_index_groups=chips)
    new_master, new_one, new_two = finish(mean_grad, master, moment_one, moment_two)
    moved, new_master, new_one, new_two = lax.optimization_barrier((moved, new_master, new_one, new_two))
    rollout = lax.all_gather(moved.reshape(fresh.shape), REP, axis=1, tiled=True, axis_index_groups=chips)
    return (new_master, new_one, new_two, rollout)


def solution(mesh):
    devices = mesh.devices.reshape(2, 4, 2, 8, 4)
    chips = Mesh(devices, ("y_hi", "x", "core", "z", "y_lo"))
    rep = ("y_hi", "x", "core")
    placed = (P(rep, FSDP, None), P(FSDP, None), P(FSDP, None), P(FSDP, None))
    return jax.shard_map(
        local,
        mesh=chips,
        in_specs=placed,
        out_specs=(P(FSDP, None), P(FSDP, None), P(FSDP, None), P(None, FSDP)),
        check_vma=False,
    )
```

```python
import jax
import jax.numpy as jnp
from jax import lax
from jax.sharding import Mesh
from jax.sharding import PartitionSpec as P

STEP = 10
FSDP = ("z", "y_lo")
BF16, F32 = jnp.bfloat16, jnp.float32
REP = ("y_hi", "x", "core")


def half_of(place):
    return (place + place // 2 + place // 8) % 2


def adamw(mean_grad, master, moment_one, moment_two):
    new_one = 0.9 * moment_one + 0.1 * mean_grad
    new_two = 0.95 * moment_two + 0.05 * mean_grad * mean_grad
    corrected_one = new_one * (1.0 / (1.0 - 0.9**STEP))
    corrected_two = new_two * (1.0 / (1.0 - 0.95**STEP))
    new_master = master - 0.02 * (corrected_one / (jnp.sqrt(corrected_two) + 1e-08) + 0.1 * master)
    return (new_master, new_one, new_two)


def local(grads, master, moment_one, moment_two):
    rows, width = master.shape
    owners = lax.axis_size(FSDP)
    rep_count = lax.axis_size(REP)
    piece = width // owners
    part = piece // 2
    first = half_of(lax.axis_index(REP)) == 0

    def blocks(source):
        return source.reshape(source.shape[:-1] + (owners, piece))

    def half(source):
        return jnp.where(first, source[..., :part], source[..., part:])

    chips = blocks(lax.all_gather(grads[0].astype(BF16), "core"))
    total = half(chips).astype(F32).sum(0).astype(BF16).transpose(1, 0, 2)
    for step in zip((3, 7, 9), (9, 3, 7)):
        pairs = [[i, i ^ step[half_of(i)]] for i in range(rep_count) if i < i ^ step[half_of(i)]]
        lines = lax.all_gather(total, REP, axis_index_groups=pairs)
        total = lines.astype(F32).sum(0).astype(BF16)
    mean_half = lines.astype(F32).sum(0) / rep_count

    masters, firsts, seconds = blocks(master), blocks(moment_one), blocks(moment_two)
    fresh, _, _ = adamw(mean_half.transpose(1, 0, 2), half(masters), half(firsts), half(seconds))
    moved = lax.all_to_all(fresh.astype(BF16).transpose(1, 0, 2), FSDP, split_axis=0, concat_axis=0, tiled=True)
    chips = [[i + half_of(i), i + 1 - half_of(i)] for i in range(0, rep_count, 2)]
    mean_grad = lax.all_gather(mean_half, REP, axis_index_groups=chips).transpose(0, 2, 1, 3)
    mean_grad = jnp.concatenate([mean_grad[0], mean_grad[1]], -1)
    news = adamw(mean_grad, masters, firsts, seconds)
    new_master, new_one, new_two = (new.reshape(rows, width) for new in news)
    moved, new_master, new_one, new_two = lax.optimization_barrier((moved, new_master, new_one, new_two))
    rollout = lax.all_gather(moved.reshape(owners * rows, part), REP, axis=1, tiled=True, axis_index_groups=chips)
    return (new_master, new_one, new_two, rollout)


def solution(mesh):
    devices = mesh.devices.reshape(2, 4, 2, 8, 4)
    chips = Mesh(devices, ("y_hi", "x", "core", "z", "y_lo"))
    rep = ("y_hi", "x", "core")
    placed = (P(rep, FSDP, None), P(FSDP, None), P(FSDP, None), P(FSDP, None))
    return jax.shard_map(
        local,
        mesh=chips,
        in_specs=placed,
        out_specs=(P(FSDP, None), P(FSDP, None), P(FSDP, None), P(None, FSDP)),
        check_vma=False,
    )
```

```python
import jax
import jax.numpy as jnp
from jax import lax
from jax.experimental import pallas as pl
from jax.experimental.pallas import tpu as pltpu
from jax.sharding import Mesh
from jax.sharding import PartitionSpec as P

STEP = 10
FSDP = ("z", "y_lo")
BF16, F32 = jnp.bfloat16, jnp.float32


def adamw(mean_grad, master, moment_one, moment_two):
    new_one = 0.9 * moment_one + 0.1 * mean_grad
    new_two = 0.95 * moment_two + 0.05 * mean_grad * mean_grad
    corrected_one = new_one * (1.0 / (1.0 - 0.9**STEP))
    corrected_two = new_two * (1.0 / (1.0 - 0.95**STEP))
    new_master = master - 0.02 * (corrected_one / (jnp.sqrt(corrected_two) + 1e-08) + 0.1 * master)
    return (new_master, new_one, new_two)


VMEM = pl.BlockSpec(memory_space=pltpu.VMEM)
REP = ("y_hi", "x", "core")


def half_of(place):
    return (place + place // 2 + place // 8) % 2


def own_half():
    return (lax.axis_index("core") + lax.axis_index("x") + lax.axis_index("y_hi")) % 2


def combine(chips, owners):
    cores, rows, width = chips.shape
    part = width // owners // cores

    def kernel(chips_ref, sum_ref):
        half = own_half()
        for owner in range(0, owners, 2):
            sums = []
            for k in range(2):
                columns = pl.ds(pl.multiple_of((cores * (owner + k) + half) * part, part), part)
                sums.append(chips_ref[0, :, columns].astype(F32) + chips_ref[1, :, columns].astype(F32))
            sum_ref[owner * rows : (owner + 2) * rows, :] = jnp.concatenate(sums, 0).astype(BF16)

    return pl.pallas_call(
        kernel,
        in_specs=[VMEM],
        out_specs=VMEM,
        out_shape=jax.ShapeDtypeStruct((owners * rows, part), BF16),
        compiler_params=pltpu.CompilerParams(vmem_limit_bytes=8 * 2**20),
        cost_estimate=pl.CostEstimate(flops=rows * width, bytes_accessed=5 * rows * width, transcendentals=0),
        name="combine",
    )(chips)


def begin(lines, master, moment_one, moment_two, rep_count):
    rows, width = master.shape
    _, tall, part = lines.shape
    owners = tall // rows
    cores = width // part // owners

    def kernel(lines_ref, master_ref, one_ref, two_ref, fresh_ref, mean_ref):
        half = own_half()
        for owner in range(0, owners, 2):
            pair = slice(owner * rows, (owner + 2) * rows)
            mean_grad = (lines_ref[0, pair, :].astype(F32) + lines_ref[1, pair, :].astype(F32)) / rep_count
            mean_ref[pair, :] = mean_grad
            news = []
            for k in range(2):
                columns = pl.ds(pl.multiple_of((cores * (owner + k) + half) * part, part), part)
                new_master, _, _ = adamw(
                    mean_grad[k * rows : (k + 1) * rows],
                    master_ref[:, columns],
                    one_ref[:, columns],
                    two_ref[:, columns],
                )
                news.append(new_master)
            fresh_ref[pair, :] = jnp.concatenate(news, 0).astype(BF16)

    return pl.pallas_call(
        kernel,
        in_specs=[VMEM] * 4,
        out_specs=[VMEM] * 2,
        out_shape=[jax.ShapeDtypeStruct((tall, part), BF16), jax.ShapeDtypeStruct((tall, part), F32)],
        compiler_params=pltpu.CompilerParams(vmem_limit_bytes=16 * 2**20),
        cost_estimate=pl.CostEstimate(
            flops=20 * tall * part, bytes_accessed=20 * tall * part, transcendentals=tall * part
        ),
        name="begin",
    )(lines, master, moment_one, moment_two)


def finish(mean_grad, master, moment_one, moment_two):
    rows, width = master.shape
    cores, _, part = mean_grad.shape
    owners = width // part // cores
    steps = 4
    each = owners // steps

    def kernel(mean_ref, master_ref, one_ref, two_ref, *refs):
        outs, (held, sems) = refs[:3], refs[3:]
        copies = []
        for step in range(steps):
            for owner in range(step * each, (step + 1) * each):
                for place in range(cores):
                    columns = slice((cores * owner + place) * part, (cores * owner + place + 1) * part)
                    news = adamw(
                        mean_ref[place, owner * rows : (owner + 1) * rows, :],
                        master_ref[:, columns],
                        one_ref[:, columns],
                        two_ref[:, columns],
                    )
                    for k in range(3):
                        held[k, :, columns] = news[k]
            span = pl.ds(step * width // steps, width // steps)
            for k in range(3):
                copy = pltpu.make_async_copy(held.at[k, :, span], outs[k].at[:, span], sems.at[step, k])
                copy.start()
                copies.append(copy)
        for copy in copies:
            copy.wait()

    return pl.pallas_call(
        kernel,
        in_specs=[VMEM] * 4,
        out_specs=[pl.BlockSpec(memory_space=pl.ANY)] * 3,
        out_shape=[jax.ShapeDtypeStruct((rows, width), F32)] * 3,
        scratch_shapes=[pltpu.VMEM((3, rows, width), F32), pltpu.SemaphoreType.DMA((steps, 3))],
        compiler_params=pltpu.CompilerParams(vmem_limit_bytes=16 * 2**20),
        cost_estimate=pl.CostEstimate(
            flops=20 * rows * width, bytes_accessed=7 * 4 * rows * width, transcendentals=rows * width
        ),
        name="finish",
    )(mean_grad, master, moment_one, moment_two)


def local(grads, master, moment_one, moment_two):
    rows, width = master.shape
    owners = lax.axis_size(FSDP)
    cores = lax.axis_size("core")
    rep_count = cores * lax.axis_size("x") * lax.axis_size("y_hi")
    total = combine(lax.all_gather(grads[0].astype(BF16), "core"), owners)
    for step in zip((3, 7, 9), (9, 3, 7)):
        pairs = [[i, i ^ step[half_of(i)]] for i in range(rep_count) if i < i ^ step[half_of(i)]]
        lines = lax.all_gather(total, REP, axis_index_groups=pairs)
        total = lines.astype(F32).sum(0).astype(BF16)

    fresh, mean_half = begin(lines, master, moment_one, moment_two, rep_count)
    moved = lax.all_to_all(fresh.reshape(owners, rows, -1), FSDP, split_axis=0, concat_axis=0, tiled=True)
    chips = [[i + half_of(i), i + 1 - half_of(i)] for i in range(0, rep_count, 2)]
    mean_grad = lax.all_gather(mean_half, REP, axis_index_groups=chips)
    new_master, new_one, new_two = finish(mean_grad, master, moment_one, moment_two)
    moved, new_master, new_one, new_two = lax.optimization_barrier((moved, new_master, new_one, new_two))
    sides = lax.all_gather(moved.reshape(fresh.shape), REP, axis_index_groups=chips)
    rollout = jnp.concatenate([sides[0], sides[1]], 1)
    return (new_master, new_one, new_two, rollout)


def solution(mesh):
    devices = mesh.devices.reshape(2, 4, 2, 8, 4)
    chips = Mesh(devices, ("y_hi", "x", "core", "z", "y_lo"))
    rep = ("y_hi", "x", "core")
    placed = (P(rep, FSDP, None), P(FSDP, None), P(FSDP, None), P(FSDP, None))
    return jax.shard_map(
        local,
        mesh=chips,
        in_specs=placed,
        out_specs=(P(FSDP, None), P(FSDP, None), P(FSDP, None), P(None, FSDP)),
        check_vma=False,
    )
```
